1024 devices in a mesh: op: 4 (over x), vp: 16 (over z), cd: 16 (over y, core).
Axes of the slice: x: 4, y: 8, z: 16, core: 2. Of those that a mesh axis runs over, the one named last changes fastest.
Arguments:
- t2_amps: float32 [1024, 65536], P(('op', 'vp'), 'cd'), may hold values from -16 to 16
- w_slab: float32 [16384, 32768], P('vp', 'cd'), may hold values from -0.0625 to 0.0625
- irrep_ab: int32 [16384], replicated, may hold values from 0 to 7, as said below
- irrep_cd: int32 [65536], P('cd'), may hold values from 0 to 7, as said below
Outputs:
- ladder: float32 [1024, 16384], P(('op', 'cd'), 'vp')
The draws below stay inside these ranges and needn't reach their ends.
Inputs may be any that keep to these rules, and one draw needn't show every extreme that they name: `irrep_ab`: within the rows of each owner (aligned blocks of 1024) nondecreasing and taking exactly two consecutive values. `irrep_cd`: within each aligned block of 4096 nondecreasing and taking every value; each value on at most 1024 entries of a block, and in every block two consecutive values have exactly 1024 entries each.
All inputs are finite; a program needn't handle non-finite values.
Results may differ from the reference program's by a relative error of at most 0.0003.
Values sent between devices are 32-bit elements; how exact they have to be, the bound alone decides.
No kernel may reach another device: no remote copies, remote signals or barrier semaphores. Data moves between devices by JAX's collectives and lax.ppermute only.
A program may use at most 32 MiB of HBM per device.

```python
import jax
import jax.numpy as jnp
from jax import lax

AB_DEV = 1024
CD_DEV = 4096
IRREPS = 8
WIN = 2048
IJ = 1024
AB = 16384
CD = 65536
CD_KEPT = 32768
N_VP = 16
N_CD = 16


def block_labels(key):
    key_pair, key_weights = jax.random.split(key)
    quarter = CD_DEV // 4
    rest = CD_DEV - 2 * quarter
    others_count = IRREPS - 2
    pair_start = jax.random.randint(key_pair, (), 0, IRREPS - 1)
    weights = jax.random.randint(key_weights, (IRREPS,), 1, 5)
    places = jnp.arange(IRREPS, dtype=jnp.int32)
    others = jnp.logical_and(places != pair_start, places != pair_start + 1).astype(jnp.int32)
    total_weight = jnp.sum(weights * others)
    base = 1 + (rest - others_count) * weights // total_weight
    remain = rest - jnp.sum(base * others)
    ordinal = jnp.cumsum(others) - 1
    extra = (ordinal < remain).astype(jnp.int32)
    sizes = jnp.where(others == 1, base + extra, quarter)
    bounds = jnp.cumsum(sizes)[:-1]
    positions = jnp.arange(CD_DEV, dtype=jnp.int32)
    return jnp.sum((positions[:, None] >= bounds[None, :]).astype(jnp.int32), axis=1)


def draw_irrep_cd(key, part):
    key = jax.random.fold_in(key, 23)
    keys = jax.random.split(key, N_CD)
    return jax.vmap(block_labels)(keys).reshape(-1).astype(jnp.int32)


def owner_irreps(key):
    key_low, key_split = jax.random.split(key)
    low = jax.random.randint(key_low, (), 0, IRREPS - 1)
    split = jax.random.randint(key_split, (), 1, AB_DEV)
    positions = jnp.arange(AB_DEV, dtype=jnp.int32)
    return low + (positions >= split).astype(jnp.int32)


def draw_irrep_ab(key, part):
    key = jax.random.fold_in(key, 11)
    keys = jax.random.split(key, N_VP)
    return jax.vmap(owner_irreps)(keys).reshape(-1).astype(jnp.int32)


def raised(array, own_key, source, target, blocks, factor):
    owner, partner = [(jnp.arange(array.shape[position]) // (array.shape[position] // blocks)).reshape([-1 if axis == position else 1 for axis in range(array.ndim)]) for position in (source, target)]
    chosen = jax.random.permutation(own_key, blocks)[partner]
    strong = (owner == chosen) | (owner == (partner + blocks // 2) % blocks)
    return jnp.where(strong, factor * array, array)


def level_of(own_key, extent, cuts, least, high):
    factor_of, own = 1.0, jax.random.fold_in(own_key, 6)
    for position, shards_of in cuts:
        draws = jnp.exp(jax.random.uniform(jax.random.fold_in(own, position), (shards_of,), jnp.float32, least / len(cuts), high / len(cuts)))
        factor_of = factor_of * jnp.repeat(draws, extent[position] // shards_of).reshape([-1 if axis == position else 1 for axis in range(len(extent))])
    return factor_of


def scatter_about(rng, dims, deviation, bound, shards=(), kind=jnp.bfloat16):
    values = deviation * jax.random.normal(rng, dims, jnp.float32)
    if shards:
        values = values * level_of(rng, dims, shards, -0.22, 0.18)
    return jnp.clip(values, -bound, bound).astype(kind)


def bell_draw_with(own_key, shape, deviation, reach, pieces, heavy, kind=jnp.bfloat16):
    entries = deviation * jax.random.normal(own_key, shape, jnp.float32)
    if pieces:
        entries = entries * level_of(own_key, shape, pieces, -0.22, 0.18)
    return jnp.clip(raised(entries, jax.random.fold_in(own_key, 3), *heavy), -reach, reach).astype(kind)


def setup_inputs(seed: int = 0) -> dict:
    arg_keys = jax.random.split(jax.random.key(seed), 5)
    return {
        "t2_amps": bell_draw_with(arg_keys[0], (IJ, CD), 1.0, 16.0, ((0, 64), (1, 16)), (1, 0, 64, 4.0), jnp.float32),
        "w_slab": scatter_about(arg_keys[1], (AB, CD_KEPT), (CD // IRREPS) ** -0.5, 0.0625, ((0, 16), (1, 16)), jnp.float32),
        "irrep_ab": draw_irrep_ab(jax.random.fold_in(arg_keys[4], 71), 0),
        "irrep_cd": draw_irrep_cd(jax.random.fold_in(arg_keys[4], 71), 0),
    }


def reference(t2_amps, w_slab, irrep_ab, irrep_cd):
    cd_blocks = irrep_cd.reshape(N_CD, CD_DEV)
    label_rows = irrep_ab.reshape(N_VP, AB_DEV)
    lows = label_rows[:, 0]

    def one_owner(triple):
        w_block, lab_block, low = triple
        counts = jnp.sum((cd_blocks < low).astype(jnp.int32), axis=1).astype(jnp.int32)
        starts = jnp.minimum(counts, CD_DEV - WIN).astype(jnp.int32)
        columns = (jnp.arange(N_CD, dtype=jnp.int32)[:, None] * CD_DEV + starts[:, None] + jnp.arange(WIN, dtype=jnp.int32)[None, :]).reshape(-1).astype(jnp.int32)
        amps = jnp.take(t2_amps, columns, axis=1)
        labels = jnp.take(irrep_cd, columns)
        masked = jnp.where(lab_block[:, None] == labels[None, :], w_block, jnp.zeros_like(w_block))
        return lax.dot_general(amps, masked, (((1,), (1,)), ((), ())), precision=lax.Precision.HIGHEST, preferred_element_type=jnp.float32)

    result = lax.map(one_owner, (w_slab.reshape(N_VP, AB_DEV, CD_KEPT), label_rows, lows))
    return jnp.transpose(result, (1, 0, 2)).reshape(IJ, AB)
```

```python
import jax
import jax.numpy as jnp
from jax import lax
from jax.sharding import PartitionSpec as P


def contract(amps, masked):
    return lax.dot_general(
        amps,
        masked,
        (((1,), (1,)), ((), ())),
        precision=lax.Precision.HIGH,
        preferred_element_type=jnp.float32,
    )


def reduce_rows(partial_rows):
    n_cd = lax.axis_size("cd")
    rows, cols = partial_rows.shape
    share = rows // n_cd
    core = lax.axis_index("cd") % 2
    blocks = partial_rows.reshape(n_cd // 2, 2, share, cols)
    mine = lax.dynamic_index_in_dim(blocks, core, 1, keepdims=False)
    other = lax.dynamic_index_in_dim(blocks, 1 - core, 1, keepdims=False)
    pair = [(i, i ^ 1) for i in range(n_cd)]
    both = mine + lax.ppermute(other, "cd", pair)
    groups = [[c for c in range(n_cd) if c % 2 == p] for p in range(2)]
    parts = lax.all_to_all(both, "cd", 0, 0, axis_index_groups=groups)
    return jnp.sum(parts, axis=0)


def per_device(t2_amps, w_slab, irrep_ab, irrep_cd):
    ab_dev = w_slab.shape[0]
    width = w_slab.shape[1]
    cd_dev = irrep_cd.shape[0]
    own = lax.axis_index("vp")
    own_labels = lax.dynamic_slice_in_dim(irrep_ab, own * ab_dev, ab_dev, 0)
    count = jnp.sum((irrep_cd < own_labels[0]).astype(jnp.int32))
    own_start = jnp.minimum(count, cd_dev - width)
    col_labels = lax.dynamic_slice_in_dim(irrep_cd, own_start, width, 0)
    masked = jnp.where(own_labels[:, None] == col_labels[None, :], w_slab, jnp.zeros_like(w_slab))
    amps_group = lax.dynamic_slice_in_dim(
        lax.all_gather(t2_amps, "vp", axis=0, tiled=True), own_start, width, 1
    )
    return reduce_rows(contract(amps_group, masked))


def solution(mesh):
    placed = (P(("op", "vp"), "cd"), P("vp", "cd"), P(), P("cd"))
    return jax.shard_map(
        per_device, mesh=mesh, in_specs=placed, out_specs=P(("op", "cd"), "vp"), check_vma=False
    )
```

```python
import functools

import jax
import jax.numpy as jnp
from jax import lax
from jax.experimental import pallas as pl
from jax.experimental.pallas import tpu as pltpu
from jax.sharding import PartitionSpec as P

LANES = 128
AB_TILE = 256


def contract_kernel(rels, shapes, width, carried, scal, *refs):
    n_src = len(shapes)
    srcs, refs = refs[:n_src], refs[n_src:]
    w_ref, refs = refs[0], refs[1:]
    if carried:
        old_mine, old_other, refs = refs[0], refs[1], refs[2:]
    mine, other, hi, lo = refs
    tile0, off, n_low, a0, a1, a2, z, d, core = [scal[i] for i in range(9)]
    step = pl.program_id(0)
    tiles = width // LANES
    share = hi.shape[0] // len(rels)

    @pl.when(step == 0)
    def build():
        lane = lax.broadcasted_iota(jnp.int32, (share, LANES), 1)
        keep = lane < LANES - off
        turn = lax.rem(LANES - off, LANES)
        row = 0
        for ref, count in zip(srcs, shapes):
            for i in range(1 if count is None else count):
                rolled = None
                for j in range(tiles + 1):
                    if count is None:
                        piece = ref[:, pl.ds(tile0 + j, 1)]
                    else:
                        piece = ref[i, :, pl.ds(j, 1)]
                    piece = piece.reshape(share, LANES)
                    new = pltpu.roll(piece, turn, 1)
                    if rolled is not None:
                        value = jnp.where(keep, rolled, new)
                        high = value.astype(jnp.bfloat16)
                        rest = (value - high.astype(jnp.float32)).astype(jnp.bfloat16)
                        at = (slice(row, row + share), slice((j - 1) * LANES, j * LANES))
                        hi[at] = high
                        lo[at] = rest
                    rolled = new
                row += share

    rows = lax.broadcasted_iota(jnp.int32, (AB_TILE, 1), 0) + step * AB_TILE
    first = jnp.where(rows < n_low, a0, a1)
    last = jnp.where(rows < n_low, a1, a2)
    cols = lax.broadcasted_iota(jnp.int32, (AB_TILE, width), 1)
    w = jnp.where((cols >= first) & (cols < last), w_ref[...], 0.0)
    w_hi = w.astype(jnp.bfloat16)
    w_lo = (w - w_hi.astype(jnp.float32)).astype(jnp.bfloat16)
    dot = functools.partial(
        lax.dot_general,
        dimension_numbers=(((1,), (1,)), ((), ())),
        preferred_element_type=jnp.float32,
    )
    out = dot(hi[...], w_lo) + dot(lo[...], w_hi) + dot(hi[...], w_hi)
    if carried:
        mine[...] = old_mine[...]
        other[...] = old_other[...]
    for i, rel in enumerate(rels):
        block = (z + rel * d + 32) & 15
        value = out[i * share : (i + 1) * share]

        @pl.when((block & 1) == core)
        def keep_block():
            mine[pl.ds(block >> 1, 1)] = value[None]

        @pl.when((block & 1) != core)
        def send_block():
            other[pl.ds(block >> 1, 1)] = value[None]


def contract(scal, sources, rels, w_slab, old=()):
    ab, width = w_slab.shape
    shapes = [None if s.ndim == 4 else s.shape[0] for s in sources]
    share = 16
    rows = share * len(rels)
    whole = [pl.BlockSpec(s.shape, functools.partial(lambda n, i: (0,) * n, s.ndim)) for s in sources]
    out_spec = pl.BlockSpec((8, share, AB_TILE), lambda i: (0, 0, i))
    out_shape = jax.ShapeDtypeStruct((8, share, ab), jnp.float32)
    return pl.pallas_call(
        functools.partial(contract_kernel, rels, shapes, width, bool(old)),
        grid=(ab // AB_TILE,),
        in_specs=[pl.BlockSpec(memory_space=pltpu.SMEM)]
        + whole
        + [pl.BlockSpec((AB_TILE, width), lambda i: (i, 0))]
        + [out_spec] * len(old),
        out_specs=[out_spec, out_spec],
        out_shape=[out_shape, out_shape],
        scratch_shapes=[pltpu.VMEM((rows, width), jnp.bfloat16)] * 2,
        compiler_params=pltpu.CompilerParams(vmem_limit_bytes=40 * 1024 * 1024),
        cost_estimate=pl.CostEstimate(
            flops=6 * rows * width * ab, bytes_accessed=4 * ab * width, transcendentals=0
        ),
    )(scal, *sources, w_slab, *old)


def reduce_rows(mine, other):
    n_cd = lax.axis_size("cd")
    pair = [(i, i ^ 1) for i in range(n_cd)]
    both = mine + lax.ppermute(other, "cd", pair)
    groups = [[c for c in range(n_cd) if c % 2 == p] for p in range(2)]
    parts = lax.all_to_all(both, "cd", 0, 0, axis_index_groups=groups)
    return jnp.sum(parts, axis=0)


def per_device(t2_amps, w_slab, irrep_ab, irrep_cd):
    n_vp = lax.axis_size("vp")
    n_cd = lax.axis_size("cd")
    ab_dev, width = w_slab.shape
    rows_dev, cd_dev = t2_amps.shape
    win_tiles = width // LANES + 1
    z = lax.axis_index("vp")
    c = lax.axis_index("cd")
    core = c % 2
    d = 1 - 2 * core

    def move(array, k):
        pairs = [
            (v * n_cd + e, ((v + (k if e % 2 == 0 else -k)) % n_vp) * n_cd + e)
            for v in range(n_vp)
            for e in range(n_cd)
        ]
        return lax.ppermute(array, ("vp", "cd"), pairs)

    labels = irrep_ab.reshape(n_vp, ab_dev)
    lows = labels[:, 0]
    counts = jnp.sum((irrep_cd[None, :] < lows[:, None]).astype(jnp.int32), axis=1)
    starts = jnp.minimum(counts, cd_dev - width)
    tile_of = jnp.minimum(starts // LANES, cd_dev // LANES - win_tiles)
    low = lows[z]
    start = starts[z]
    tile0 = tile_of[z]
    below1 = jnp.sum((irrep_cd <= low).astype(jnp.int32))
    below2 = jnp.sum((irrep_cd <= low + 1).astype(jnp.int32))
    n_low = jnp.sum((labels[z] == low).astype(jnp.int32))
    scal = jnp.stack(
        [tile0, start - tile0 * LANES, n_low, counts[z] - start, below1 - start, below2 - start, z, d, core]
    ).astype(jnp.int32)

    def window(block, k):
        at = tile_of[(z + k * d + 2 * n_vp) % n_vp]
        return lax.dynamic_slice(block, (0, at, 0, 0), (block.shape[0], win_tiles, 8, LANES))

    own = t2_amps.reshape(rows_dev // 8, 8, cd_dev // LANES, LANES).transpose(0, 2, 1, 3)
    x1 = move(own, 3)
    y1 = move(own, -3)
    x2 = move(x1, 3)
    y2 = move(y1, -3)
    near_x = move(jnp.stack([window(b, 1) for b in (own, x1, y1)]), 1)
    near_y = move(jnp.stack([window(b, -1) for b in (own, x1, y1)]), -1)
    far_x = move(jnp.stack([window(b, 1) for b in (x2, y2)]), 1)
    far_y = move(jnp.stack([window(b, -1) for b in (x2, y2)]), -1)
    edge = move(window(x2, 2)[None], 2)
    first = contract(
        scal,
        [own, x1, y1, x2, y2, near_x, near_y],
        [0, -3, 3, -6, 6, -1, -4, 2, 1, -2, 4],
        w_slab,
    )
    mine, other = contract(scal, [far_x, far_y, edge], [-7, 5, -5, 7, -8], w_slab, first)
    return reduce_rows(mine, other)


def solution(mesh):
    placed = (P(("op", "vp"), "cd"), P("vp", "cd"), P(), P("cd"))
    return jax.shard_map(
        per_device, mesh=mesh, in_specs=placed, out_specs=P(("op", "cd"), "vp"), check_vma=False
    )
```

```python
import functools

import jax
import jax.numpy as jnp
from jax import lax
from jax.experimental import pallas as pl
from jax.experimental.pallas import tpu as pltpu
from jax.sharding import PartitionSpec as P

LANES = 128
AB_TILE = 256
IRREPS = 8
OFF, N_LOW, COL0, COL1, COL2, TILE = 0, 1, 2, 3, 4, 5


def position():
    z = lax.axis_index("vp")
    core = lax.axis_index("cd") & 1
    return z, core, 1 - 2 * core


def prepare_kernel(owners, win_tiles, ab_ref, cd_ref, w_ref, scal, hi, lo, below):
    step = pl.program_id(0)
    width = w_ref.shape[1]
    n_cd_tiles = cd_ref.shape[0]
    per_owner = ab_ref.shape[0] // owners

    @pl.when(step == 0)
    def count():
        z, core, d = position()

        def total(mask):
            return jnp.sum(jnp.where(mask, 1.0, 0.0)).astype(jnp.int32)

        labels = cd_ref[...]
        below[0] = jnp.int32(0)
        below[IRREPS] = jnp.int32(n_cd_tiles * LANES)
        for r in range(1, IRREPS):
            below[r] = total(labels < r)

        def low_of(v):
            rows = ab_ref[pl.ds(pl.multiple_of(v * per_owner, per_owner), per_owner)]
            return jnp.min(rows.astype(jnp.float32)).astype(jnp.int32), rows

        def start_of(low):
            start = jnp.minimum(below[low], n_cd_tiles * LANES - width)
            return start, jnp.minimum(start // LANES, n_cd_tiles - win_tiles)

        low, rows = low_of(z)
        start, tile = start_of(low)
        scal[OFF] = start - tile * LANES
        scal[N_LOW] = total(rows == low)
        scal[COL0] = below[low] - start
        scal[COL1] = below[low + 1] - start
        scal[COL2] = below[low + 2] - start
        scal[TILE] = tile
        for i, k in enumerate((1, -1, 2)):
            scal[TILE + 1 + i] = start_of(low_of((z + k * d + 2 * owners) % owners)[0])[1]

    rows = lax.broadcasted_iota(jnp.int32, (AB_TILE, 1), 0) + step * AB_TILE
    first = jnp.where(rows < scal[N_LOW], scal[COL0], scal[COL1])
    last = jnp.where(rows < scal[N_LOW], scal[COL1], scal[COL2])
    for at in range(0, width, LANES):
        cols = lax.broadcasted_iota(jnp.int32, (AB_TILE, LANES), 1) + at
        w = jnp.where((cols >= first) & (cols < last), w_ref[:, at : at + LANES], 0.0)
        high = w.astype(jnp.bfloat16)
        hi[:, at : at + LANES] = high
        lo[:, at : at + LANES] = (w - high.astype(jnp.float32)).astype(jnp.bfloat16)


def prepare(irrep_ab, irrep_cd, w_slab, owners):
    ab, width = w_slab.shape
    labels_ab = irrep_ab.reshape(-1, LANES)
    labels_cd = irrep_cd.reshape(-1, LANES)
    tile_spec = pl.BlockSpec((AB_TILE, width), lambda i: (i, 0))
    half = jax.ShapeDtypeStruct((ab, width), jnp.bfloat16)
    return pl.pallas_call(
        functools.partial(prepare_kernel, owners, width // LANES + 1),
        grid=(ab // AB_TILE,),
        in_specs=[
            pl.BlockSpec(labels_ab.shape, lambda i: (0, 0)),
            pl.BlockSpec(labels_cd.shape, lambda i: (0, 0)),
            tile_spec,
        ],
        out_specs=[pl.BlockSpec(memory_space=pltpu.SMEM), tile_spec, tile_spec],
        out_shape=[jax.ShapeDtypeStruct((16,), jnp.int32), half, half],
        scratch_shapes=[pltpu.SMEM((16,), jnp.int32)],
        compiler_params=pltpu.CompilerParams(vmem_limit_bytes=24 * 1024 * 1024),
        cost_estimate=pl.CostEstimate(flops=8 * ab * width, bytes_accessed=8 * ab * width, transcendentals=0),
    )(labels_ab, labels_cd, w_slab)


def cut_kernel(picks, n_src, scal, *refs):
    srcs, outs = refs[:n_src], refs[n_src:]
    for out, (place, chosen) in zip(outs, picks):
        at = scal[TILE + place]
        for i, s in enumerate(chosen):
            out[i] = srcs[s][:, pl.ds(at, out.shape[2])]


def cut(scal, sources, picks, win_tiles):
    groups, _, _, _ = sources[0].shape
    outs = [jax.ShapeDtypeStruct((len(p[1]), groups, win_tiles, 8, LANES), jnp.float32) for p in picks]
    vmem = pl.BlockSpec(memory_space=pltpu.VMEM)
    size = sum(4 * o.size for o in outs)
    return pl.pallas_call(
        functools.partial(cut_kernel, picks, len(sources)),
        in_specs=[pl.BlockSpec(memory_space=pltpu.SMEM)] + [vmem] * len(sources),
        out_specs=[vmem] * len(outs),
        out_shape=outs,
        compiler_params=pltpu.CompilerParams(vmem_limit_bytes=8 * 1024 * 1024),
        cost_estimate=pl.CostEstimate(flops=0, bytes_accessed=2 * size, transcendentals=0),
    )(scal, *sources)


def contract_kernel(rels, shapes, carried, scal, *refs):
    n_src = len(shapes)
    srcs, refs = refs[:n_src], refs[n_src:]
    w_hi, w_lo, refs = refs[0], refs[1], refs[2:]
    if carried:
        old_mine, old_other, refs = refs[0], refs[1], refs[2:]
    mine, other, amps = refs
    width = w_hi.shape[1]
    padded = amps.shape[1] // 2
    tiles = width // LANES
    share = mine.shape[1]

    @pl.when(pl.program_id(0) == 0)
    def build():
        off, tile0 = scal[OFF], scal[TILE]
        lane = lax.broadcasted_iota(jnp.int32, (padded, LANES), 1)
        keep = lane < LANES - off
        turn = lax.rem(LANES - off, LANES)
        rolled = None
        for j in range(tiles + 1):
            pieces = []
            for ref, count in zip(srcs, shapes):
                if count is None:
                    pieces.append(ref[:, pl.ds(tile0 + j, 1)].reshape(share, LANES))
                else:
                    pieces += [ref[i, :, j].reshape(share, LANES) for i in range(count)]
            if padded > share * len(rels):
                pieces.append(jnp.zeros((padded - share * len(rels), LANES), jnp.float32))
            new = pltpu.roll(jnp.concatenate(pieces, axis=0), turn, 1)
            if rolled is not None:
                value = jnp.where(keep, rolled, new).T
                high = value.astype(jnp.bfloat16)
                rows = slice((j - 1) * LANES, j * LANES)
                amps[rows, :padded] = high
                amps[rows, padded:] = (value - high.astype(jnp.float32)).astype(jnp.bfloat16)
            rolled = new

    dot = functools.partial(jnp.dot, preferred_element_type=jnp.float32)
    both = dot(w_hi[...], amps[...])
    turned = both[:, :padded] + both[:, padded:] + dot(w_lo[...], amps[:, :padded])
    out = turned.T
    if carried:
        mine[...] = old_mine[...]
        other[...] = old_other[...]
    z, core, d = position()
    for i, rel in enumerate(rels):
        block = (z + rel * d + 32) & 15
        value = out[i * share : (i + 1) * share]

        @pl.when((block & 1) == core)
        def keep_block():
            mine[pl.ds(block >> 1, 1)] = value[None]

        @pl.when((block & 1) != core)
        def send_block():
            other[pl.ds(block >> 1, 1)] = value[None]


def contract(scal, sources, rels, w_hi, w_lo, old=()):
    ab, width = w_hi.shape
    shapes = [None if s.ndim == 4 else s.shape[0] for s in sources]
    share = 16
    rows = share * len(rels)
    padded = -(-rows // LANES) * LANES
    whole = [pl.BlockSpec(s.shape, functools.partial(lambda n, i: (0,) * n, s.ndim)) for s in sources]
    tile_spec = pl.BlockSpec((AB_TILE, width), lambda i: (i, 0))
    out_spec = pl.BlockSpec((8, share, AB_TILE), lambda i: (0, 0, i))
    out_shape = jax.ShapeDtypeStruct((8, share, ab), jnp.float32)
    return pl.pallas_call(
        functools.partial(contract_kernel, rels, shapes, bool(old)),
        grid=(ab // AB_TILE,),
        in_specs=[pl.BlockSpec(memory_space=pltpu.SMEM)] + whole + [tile_spec] * 2 + [out_spec] * len(old),
        out_specs=[out_spec, out_spec],
        out_shape=[out_shape, out_shape],
        scratch_shapes=[pltpu.VMEM((width, 2 * padded), jnp.bfloat16)],
        compiler_params=pltpu.CompilerParams(vmem_limit_bytes=24 * 1024 * 1024),
        cost_estimate=pl.CostEstimate(
            flops=6 * rows * width * ab, bytes_accessed=4 * ab * width, transcendentals=0
        ),
    )(scal, *sources, w_hi, w_lo, *old)


def reduce_rows(mine, other):
    n_cd = lax.axis_size("cd")
    pair = [(i, i ^ 1) for i in range(n_cd)]
    both = mine + lax.ppermute(other, "cd", pair)
    groups = [[c for c in range(n_cd) if c % 2 == p] for p in range(2)]
    parts = lax.all_to_all(both, "cd", 0, 0, axis_index_groups=groups)
    return jnp.sum(parts, axis=0)


def per_device(t2_amps, w_slab, irrep_ab, irrep_cd):
    n_vp = lax.axis_size("vp")
    n_cd = lax.axis_size("cd")
    rows_dev, cd_dev = t2_amps.shape
    win_tiles = w_slab.shape[1] // LANES + 1

    def move(array, k):
        pairs = [
            (v * n_cd + e, ((v + (k if e % 2 == 0 else -k)) % n_vp) * n_cd + e)
            for v in range(n_vp)
            for e in range(n_cd)
        ]
        return lax.ppermute(array, ("vp", "cd"), pairs)

    own = t2_amps.reshape(rows_dev // 8, 8, cd_dev // LANES, LANES).transpose(0, 2, 1, 3)
    x1 = move(own, 3)
    y1 = move(own, -3)
    scal, w_hi, w_lo = prepare(irrep_ab, irrep_cd, w_slab, n_vp)
    x2 = move(x1, 3)
    y2 = move(y1, -3)
    to_x, to_y = cut(scal, [own, x1, y1], [(1, (0, 1, 2)), (2, (0, 1, 2))], win_tiles)
    near_x = move(to_x, 1)
    near_y = move(to_y, -1)
    to_x, to_y, to_edge = cut(scal, [x2, y2], [(1, (0, 1)), (2, (0, 1)), (3, (0,))], win_tiles)
    far_x = move(to_x, 1)
    far_y = move(to_y, -1)
    edge = move(to_edge, 2)
    first = contract(
        scal,
        [own, x1, y1, x2, y2, near_x, near_y],
        [0, -3, 3, -6, 6, -1, -4, 2, 1, -2, 4],
        w_hi,
        w_lo,
    )
    mine, other = contract(scal, [far_x, far_y, edge], [-7, 5, -5, 7, -8], w_hi, w_lo, first)
    return reduce_rows(mine, other)


def solution(mesh):
    placed = (P(("op", "vp"), "cd"), P("vp", "cd"), P(), P("cd"))
    return jax.shard_map(
        per_device, mesh=mesh, in_specs=placed, out_specs=P(("op", "cd"), "vp"), check_vma=False
    )
```

```python
import functools

import jax
import jax.numpy as jnp
from jax import lax
from jax.experimental import pallas as pl
from jax.experimental.pallas import tpu as pltpu
from jax.sharding import PartitionSpec as P

LANES = 128
AB_TILE = 256
IRREPS = 8
OFF, N_LOW, COL0, COL1, COL2, TILE = 0, 1, 2, 3, 4, 5


def position():
    z = lax.axis_index("vp")
    core = lax.axis_index("cd") & 1
    return z, core, 1 - 2 * core


def prepare_kernel(owners, win_tiles, ab_ref, cd_ref, w_ref, scal, hi, lo, below):
    step = pl.program_id(0)
    width = w_ref.shape[1]
    n_cd_tiles = cd_ref.shape[0]
    per_owner = ab_ref.shape[0] // owners

    @pl.when(step == 0)
    def count():
        z, core, d = position()

        def total(mask):
            return jnp.sum(jnp.where(mask, 1.0, 0.0)).astype(jnp.int32)

        labels = cd_ref[...]
        below[0] = jnp.int32(0)
        below[IRREPS] = jnp.int32(n_cd_tiles * LANES)
        for r in range(1, IRREPS):
            below[r] = total(labels < r)

        def low_of(v):
            rows = ab_ref[pl.ds(pl.multiple_of(v * per_owner, per_owner), per_owner)]
            return jnp.min(rows.astype(jnp.float32)).astype(jnp.int32), rows

        def start_of(low):
            start = jnp.minimum(below[low], n_cd_tiles * LANES - width)
            return start, jnp.minimum(start // LANES, n_cd_tiles - win_tiles)

        low, rows = low_of(z)
        start, tile = start_of(low)
        scal[OFF] = start - tile * LANES
        scal[N_LOW] = total(rows == low)
        scal[COL0] = below[low] - start
        scal[COL1] = below[low + 1] - start
        scal[COL2] = below[low + 2] - start
        scal[TILE] = tile
        for i, k in enumerate((1, -1, 2)):
            scal[TILE + 1 + i] = start_of(low_of((z + k * d + 2 * owners) % owners)[0])[1]

    rows = lax.broadcasted_iota(jnp.int32, (AB_TILE, 1), 0) + step * AB_TILE
    first = jnp.where(rows < scal[N_LOW], scal[COL0], scal[COL1])
    last = jnp.where(rows < scal[N_LOW], scal[COL1], scal[COL2])
    for at in range(0, width, LANES):
        cols = lax.broadcasted_iota(jnp.int32, (AB_TILE, LANES), 1) + at
        w = jnp.where((cols >= first) & (cols < last), w_ref[:, at : at + LANES], 0.0)
        high = w.astype(jnp.bfloat16)
        hi[:, at : at + LANES] = high
        lo[:, at : at + LANES] = (w - high.astype(jnp.float32)).astype(jnp.bfloat16)


def prepare(irrep_ab, irrep_cd, w_slab, owners):
    ab, width = w_slab.shape
    labels_ab = irrep_ab.reshape(-1, LANES)
    labels_cd = irrep_cd.reshape(-1, LANES)
    tile_spec = pl.BlockSpec((AB_TILE, width), lambda i: (i, 0))
    half = jax.ShapeDtypeStruct((ab, width), jnp.bfloat16)
    return pl.pallas_call(
        functools.partial(prepare_kernel, owners, width // LANES + 1),
        grid=(ab // AB_TILE,),
        in_specs=[
            pl.BlockSpec(labels_ab.shape, lambda i: (0, 0)),
            pl.BlockSpec(labels_cd.shape, lambda i: (0, 0)),
            tile_spec,
        ],
        out_specs=[pl.BlockSpec(memory_space=pltpu.SMEM), tile_spec, tile_spec],
        out_shape=[jax.ShapeDtypeStruct((16,), jnp.int32), half, half],
        scratch_shapes=[pltpu.SMEM((16,), jnp.int32)],
        compiler_params=pltpu.CompilerParams(vmem_limit_bytes=24 * 1024 * 1024),
        cost_estimate=pl.CostEstimate(flops=8 * ab * width, bytes_accessed=8 * ab * width, transcendentals=0),
    )(labels_ab, labels_cd, w_slab)


def cut_kernel(picks, n_src, scal, *refs):
    srcs, outs = refs[:n_src], refs[n_src:]
    for out, (place, chosen) in zip(outs, picks):
        at = scal[TILE + place]
        for i, s in enumerate(chosen):
            out[i] = srcs[s][:, pl.ds(at, out.shape[2])]


def cut(scal, sources, picks, win_tiles):
    groups, _, _, _ = sources[0].shape
    outs = [jax.ShapeDtypeStruct((len(p[1]), groups, win_tiles, 8, LANES), jnp.float32) for p in picks]
    vmem = pl.BlockSpec(memory_space=pltpu.VMEM)
    size = sum(4 * o.size for o in outs)
    return pl.pallas_call(
        functools.partial(cut_kernel, picks, len(sources)),
        in_specs=[pl.BlockSpec(memory_space=pltpu.SMEM)] + [vmem] * len(sources),
        out_specs=[vmem] * len(outs),
        out_shape=outs,
        compiler_params=pltpu.CompilerParams(vmem_limit_bytes=8 * 1024 * 1024),
        cost_estimate=pl.CostEstimate(flops=0, bytes_accessed=2 * size, transcendentals=0),
    )(scal, *sources)


def contract_kernel(rels, shapes, carried, scal, *refs):
    n_src = len(shapes)
    srcs, refs = refs[:n_src], refs[n_src:]
    w_hi, w_lo, refs = refs[0], refs[1], refs[2:]
    if carried:
        old_mine, old_other, refs = refs[0], refs[1], refs[2:]
    mine, other, amps = refs
    width = w_hi.shape[1]
    padded = amps.shape[1] // 2
    tiles = width // LANES
    share = mine.shape[1]

    @pl.when(pl.program_id(0) == 0)
    def build():
        off, tile0 = scal[OFF], scal[TILE]
        lane = lax.broadcasted_iota(jnp.int32, (padded, LANES), 1)
        keep = lane < LANES - off
        turn = lax.rem(LANES - off, LANES)
        rolled = None
        for j in range(tiles + 1):
            pieces = []
            for ref, count in zip(srcs, shapes):
                if count is None:
                    pieces.append(ref[:, pl.ds(tile0 + j, 1)].reshape(share, LANES))
                else:
                    pieces += [ref[i, :, j].reshape(share, LANES) for i in range(count)]
            if padded > share * len(rels):
                pieces.append(jnp.zeros((padded - share * len(rels), LANES), jnp.float32))
            new = pltpu.roll(jnp.concatenate(pieces, axis=0), turn, 1)
            if rolled is not None:
                value = jnp.where(keep, rolled, new).T
                high = value.astype(jnp.bfloat16)
                rows = slice((j - 1) * LANES, j * LANES)
                amps[rows, :padded] = high
                amps[rows, padded:] = (value - high.astype(jnp.float32)).astype(jnp.bfloat16)
            rolled = new

    dot = functools.partial(jnp.dot, preferred_element_type=jnp.float32)
    both = dot(w_hi[...], amps[...])
    turned = both[:, :padded] + both[:, padded:] + dot(w_lo[...], amps[:, :padded])
    out = turned.T
    if carried:
        mine[...] = old_mine[...]
        other[...] = old_other[...]
    z, core, d = position()
    for i, rel in enumerate(rels):
        block = (z + rel * d + 32) & 15
        value = out[i * share : (i + 1) * share]

        @pl.when((block & 1) == core)
        def keep_block():
            mine[pl.ds(block >> 1, 1)] = value[None]

        @pl.when((block & 1) != core)
        def send_block():
            other[pl.ds(block >> 1, 1)] = value[None]


def contract(scal, sources, rels, w_hi, w_lo, old=()):
    ab, width = w_hi.shape
    shapes = [None if s.ndim == 4 else s.shape[0] for s in sources]
    share = 16
    rows = share * len(rels)
    padded = -(-rows // LANES) * LANES
    whole = [pl.BlockSpec(s.shape, functools.partial(lambda n, i: (0,) * n, s.ndim)) for s in sources]
    tile_spec = pl.BlockSpec((AB_TILE, width), lambda i: (i, 0))
    out_spec = pl.BlockSpec((8, share, AB_TILE), lambda i: (0, 0, i))
    out_shape = jax.ShapeDtypeStruct((8, share, ab), jnp.float32)
    return pl.pallas_call(
        functools.partial(contract_kernel, rels, shapes, bool(old)),
        grid=(ab // AB_TILE,),
        in_specs=[pl.BlockSpec(memory_space=pltpu.SMEM)] + whole + [tile_spec] * 2 + [out_spec] * len(old),
        out_specs=[out_spec, out_spec],
        out_shape=[out_shape, out_shape],
        scratch_shapes=[pltpu.VMEM((width, 2 * padded), jnp.bfloat16)],
        compiler_params=pltpu.CompilerParams(vmem_limit_bytes=24 * 1024 * 1024),
        cost_estimate=pl.CostEstimate(
            flops=rows * width * ab // 8, bytes_accessed=ab * width, transcendentals=0
        ),
    )(scal, *sources, w_hi, w_lo, *old)


def reduce_rows(mine, other):
    n_cd = lax.axis_size("cd")
    pair = [(i, i ^ 1) for i in range(n_cd)]
    both = mine + lax.ppermute(other, "cd", pair)
    groups = [[c for c in range(n_cd) if c % 2 == p] for p in range(2)]
    parts = lax.all_to_all(both, "cd", 0, 0, axis_index_groups=groups)
    return jnp.sum(parts, axis=0)


def per_device(t2_amps, w_slab, irrep_ab, irrep_cd):
    n_vp = lax.axis_size("vp")
    n_cd = lax.axis_size("cd")
    rows_dev, cd_dev = t2_amps.shape
    win_tiles = w_slab.shape[1] // LANES + 1

    def move(array, k):
        pairs = [
            (v * n_cd + e, ((v + (k if e % 2 == 0 else -k)) % n_vp) * n_cd + e)
            for v in range(n_vp)
            for e in range(n_cd)
        ]
        return lax.ppermute(array, ("vp", "cd"), pairs)

    own = t2_amps.reshape(rows_dev // 8, 8, cd_dev // LANES, LANES).transpose(0, 2, 1, 3)
    x1 = move(own, 3)
    y1 = move(own, -3)
    scal, w_hi, w_lo = prepare(irrep_ab, irrep_cd, w_slab, n_vp)
    x2 = move(x1, 3)
    y2 = move(y1, -3)
    to_x, to_y = cut(scal, [own, x1, y1], [(1, (0, 1, 2)), (2, (0, 1, 2))], win_tiles)
    near_x = move(to_x, 1)
    near_y = move(to_y, -1)
    to_x, to_y, to_edge = cut(scal, [x2, y2], [(1, (0, 1)), (2, (0, 1)), (3, (0,))], win_tiles)
    far_x = move(to_x, 1)
    far_y = move(to_y, -1)
    edge = move(to_edge, 2)
    first = contract(
        scal,
        [own, x1, y1, x2, y2, near_x, near_y],
        [0, -3, 3, -6, 6, -1, -4, 2, 1, -2, 4],
        w_hi,
        w_lo,
    )
    mine, other = contract(scal, [far_x, far_y, edge], [-7, 5, -5, 7, -8], w_hi, w_lo, first)
    return reduce_rows(mine, other)


def solution(mesh):
    placed = (P(("op", "vp"), "cd"), P("vp", "cd"), P(), P("cd"))
    return jax.shard_map(
        per_device, mesh=mesh, in_specs=placed, out_specs=P(("op", "cd"), "vp"), check_vma=False
    )
```

```python
import functools

import jax
import jax.numpy as jnp
from jax import lax
from jax.experimental import pallas as pl
from jax.experimental.pallas import tpu as pltpu
from jax.sharding import PartitionSpec as P

LANES = 128
AB_TILE = 256
CONTRACT_TILE = 1024
IRREPS = 8
OFF, N_LOW, COL0, COL1, COL2, TILE = 0, 1, 2, 3, 4, 5


def position():
    z = lax.axis_index("vp")
    core = lax.axis_index("cd") & 1
    return z, core, 1 - 2 * core


def prepare_kernel(owners, win_tiles, ab_ref, cd_ref, w_ref, scal, hi, lo, below):
    step = pl.program_id(0)
    width = w_ref.shape[1]
    n_cd_tiles = cd_ref.shape[0]
    per_owner = ab_ref.shape[0] // owners

    @pl.when(step == 0)
    def count():
        z, core, d = position()

        def total(mask):
            return jnp.sum(jnp.where(mask, 1.0, 0.0)).astype(jnp.int32)

        labels = cd_ref[...]
        below[0] = jnp.int32(0)
        below[IRREPS] = jnp.int32(n_cd_tiles * LANES)
        for r in range(1, IRREPS):
            below[r] = total(labels < r)

        def low_of(v):
            rows = ab_ref[pl.ds(pl.multiple_of(v * per_owner, per_owner), per_owner)]
            return jnp.min(rows.astype(jnp.float32)).astype(jnp.int32), rows

        def start_of(low):
            start = jnp.minimum(below[low], n_cd_tiles * LANES - width)
            return start, jnp.minimum(start // LANES, n_cd_tiles - win_tiles)

        low, rows = low_of(z)
        start, tile = start_of(low)
        scal[OFF] = start - tile * LANES
        scal[N_LOW] = total(rows == low)
        scal[COL0] = below[low] - start
        scal[COL1] = below[low + 1] - start
        scal[COL2] = below[low + 2] - start
        scal[TILE] = tile
        for i, k in enumerate((1, -1, 2)):
            scal[TILE + 1 + i] = start_of(low_of((z + k * d + 2 * owners) % owners)[0])[1]

    rows = lax.broadcasted_iota(jnp.int32, (AB_TILE, 1), 0) + step * AB_TILE
    first = jnp.where(rows < scal[N_LOW], scal[COL0], scal[COL1])
    last = jnp.where(rows < scal[N_LOW], scal[COL1], scal[COL2])
    for at in range(0, width, LANES):
        cols = lax.broadcasted_iota(jnp.int32, (AB_TILE, LANES), 1) + at
        w = jnp.where((cols >= first) & (cols < last), w_ref[:, at : at + LANES], 0.0)
        high = w.astype(jnp.bfloat16)
        hi[:, at : at + LANES] = high
        lo[:, at : at + LANES] = (w - high.astype(jnp.float32)).astype(jnp.bfloat16)


def prepare(irrep_ab, irrep_cd, w_slab, owners):
    ab, width = w_slab.shape
    labels_ab = irrep_ab.reshape(-1, LANES)
    labels_cd = irrep_cd.reshape(-1, LANES)
    tile_spec = pl.BlockSpec((AB_TILE, width), lambda i: (i, 0))
    half = jax.ShapeDtypeStruct((ab, width), jnp.bfloat16)
    return pl.pallas_call(
        functools.partial(prepare_kernel, owners, width // LANES + 1),
        grid=(ab // AB_TILE,),
        in_specs=[
            pl.BlockSpec(labels_ab.shape, lambda i: (0, 0)),
            pl.BlockSpec(labels_cd.shape, lambda i: (0, 0)),
            tile_spec,
        ],
        out_specs=[pl.BlockSpec(memory_space=pltpu.SMEM), tile_spec, tile_spec],
        out_shape=[jax.ShapeDtypeStruct((16,), jnp.int32), half, half],
        scratch_shapes=[pltpu.SMEM((16,), jnp.int32)],
        compiler_params=pltpu.CompilerParams(vmem_limit_bytes=16 * 1024 * 1024),
        cost_estimate=pl.CostEstimate(flops=8 * ab * width, bytes_accessed=8 * ab * width, transcendentals=0),
    )(labels_ab, labels_cd, w_slab)


def cut_kernel(picks, n_src, scal, *refs):
    srcs, outs = refs[:n_src], refs[n_src:]
    for out, (place, chosen) in zip(outs, picks):
        at = scal[TILE + place]
        for i, s in enumerate(chosen):
            out[i] = srcs[s][:, pl.ds(at, out.shape[2])]


def cut(scal, sources, picks, win_tiles):
    groups, _, _, _ = sources[0].shape
    outs = [jax.ShapeDtypeStruct((len(p[1]), groups, win_tiles, 8, LANES), jnp.float32) for p in picks]
    vmem = pl.BlockSpec(memory_space=pltpu.VMEM)
    size = sum(4 * o.size for o in outs)
    return pl.pallas_call(
        functools.partial(cut_kernel, picks, len(sources)),
        in_specs=[pl.BlockSpec(memory_space=pltpu.SMEM)] + [vmem] * len(sources),
        out_specs=[vmem] * len(outs),
        out_shape=outs,
        compiler_params=pltpu.CompilerParams(vmem_limit_bytes=8 * 1024 * 1024),
        cost_estimate=pl.CostEstimate(flops=0, bytes_accessed=2 * size, transcendentals=0),
    )(scal, *sources)


def contract_kernel(rels, shapes, carried, scal, *refs):
    n_src = len(shapes)
    srcs, refs = refs[:n_src], refs[n_src:]
    w_hi, w_lo, refs = refs[0], refs[1], refs[2:]
    if carried:
        refs = refs[2:]
    mine, other, amps = refs
    width = w_hi.shape[1]
    padded = amps.shape[1] // 2
    tiles = width // LANES
    share = mine.shape[1]

    off, tile0 = scal[OFF], scal[TILE]
    lane = lax.broadcasted_iota(jnp.int32, (padded, LANES), 1)
    keep = lane < LANES - off
    turn = lax.rem(LANES - off, LANES)
    rolled = None
    for j in range(tiles + 1):
        pieces = []
        for ref, count in zip(srcs, shapes):
            if count is None:
                pieces.append(ref[:, pl.ds(tile0 + j, 1)].reshape(share, LANES))
            else:
                pieces += [ref[i, :, j].reshape(share, LANES) for i in range(count)]
        if padded > share * len(rels):
            pieces.append(jnp.zeros((padded - share * len(rels), LANES), jnp.float32))
        new = pltpu.roll(jnp.concatenate(pieces, axis=0), turn, 1)
        if rolled is not None:
            value = jnp.where(keep, rolled, new).T
            high = value.astype(jnp.bfloat16)
            rows = slice((j - 1) * LANES, j * LANES)
            amps[rows, :padded] = high
            amps[rows, padded:] = (value - high.astype(jnp.float32)).astype(jnp.bfloat16)
        rolled = new

    dot = functools.partial(jnp.dot, preferred_element_type=jnp.float32)
    z, core, d = position()
    for at in range(0, w_hi.shape[0], CONTRACT_TILE):
        cols = slice(at, at + CONTRACT_TILE)
        both = dot(w_hi[cols], amps[...])
        turned = both[:, :padded] + both[:, padded:] + dot(w_lo[cols], amps[:, :padded])
        out = turned.T
        for i, rel in enumerate(rels):
            block = (z + rel * d + 32) & 15
            value = out[i * share : (i + 1) * share]

            @pl.when((block & 1) == core)
            def keep_block():
                mine[pl.ds(block >> 1, 1), :, cols] = value[None]

            @pl.when((block & 1) != core)
            def send_block():
                other[pl.ds(block >> 1, 1), :, cols] = value[None]


def contract(scal, sources, rels, w_hi, w_lo, old=()):
    ab, width = w_hi.shape
    shapes = [None if s.ndim == 4 else s.shape[0] for s in sources]
    share = 16
    rows = share * len(rels)
    padded = -(-rows // LANES) * LANES
    vmem = pl.BlockSpec(memory_space=pltpu.VMEM)
    out_shape = jax.ShapeDtypeStruct((8, share, ab), jnp.float32)
    n_in = len(sources) + 3
    return pl.pallas_call(
        functools.partial(contract_kernel, rels, shapes, bool(old)),
        in_specs=[pl.BlockSpec(memory_space=pltpu.SMEM)] + [vmem] * (n_in - 1 + len(old)),
        out_specs=[vmem, vmem],
        out_shape=[out_shape, out_shape],
        input_output_aliases={n_in: 0, n_in + 1: 1} if old else {},
        scratch_shapes=[pltpu.VMEM((width, 2 * padded), jnp.bfloat16)],
        compiler_params=pltpu.CompilerParams(vmem_limit_bytes=20 * 1024 * 1024),
        cost_estimate=pl.CostEstimate(
            flops=rows * width * ab // 8, bytes_accessed=ab * width, transcendentals=0
        ),
    )(scal, *sources, w_hi, w_lo, *old)


def reduce_rows(mine, other):
    n_cd = lax.axis_size("cd")
    pair = [(i, i ^ 1) for i in range(n_cd)]
    both = mine + lax.ppermute(other, "cd", pair)
    groups = [[c for c in range(n_cd) if c % 2 == p] for p in range(2)]
    parts = lax.all_to_all(both, "cd", 0, 0, axis_index_groups=groups)
    return jnp.sum(parts, axis=0)


def per_device(t2_amps, w_slab, irrep_ab, irrep_cd):
    n_vp = lax.axis_size("vp")
    n_cd = lax.axis_size("cd")
    rows_dev, cd_dev = t2_amps.shape
    win_tiles = w_slab.shape[1] // LANES + 1

    def move(array, k):
        pairs = [
            (v * n_cd + e, ((v + (k if e % 2 == 0 else -k)) % n_vp) * n_cd + e)
            for v in range(n_vp)
            for e in range(n_cd)
        ]
        return lax.ppermute(array, ("vp", "cd"), pairs)

    own = t2_amps.reshape(rows_dev // 8, 8, cd_dev // LANES, LANES).transpose(0, 2, 1, 3)
    x1 = move(own, 3)
    y1 = move(own, -3)
    scal, w_hi, w_lo = prepare(irrep_ab, irrep_cd, w_slab, n_vp)
    x2 = move(x1, 3)
    y2 = move(y1, -3)
    to_x, to_y = cut(scal, [own, x1, y1], [(1, (0, 1, 2)), (2, (0, 1, 2))], win_tiles)
    near_x = move(to_x, 1)
    near_y = move(to_y, -1)
    to_x, to_y, to_edge = cut(scal, [x2, y2], [(1, (0, 1)), (2, (0, 1)), (3, (0,))], win_tiles)
    far_x = move(to_x, 1)
    far_y = move(to_y, -1)
    edge = move(to_edge, 2)
    first = contract(
        scal,
        [own, x1, y1, x2, y2, near_x, near_y],
        [0, -3, 3, -6, 6, -1, -4, 2, 1, -2, 4],
        w_hi,
        w_lo,
    )
    mine, other = contract(scal, [far_x, far_y, edge], [-7, 5, -5, 7, -8], w_hi, w_lo, first)
    return reduce_rows(mine, other)


def solution(mesh):
    placed = (P(("op", "vp"), "cd"), P("vp", "cd"), P(), P("cd"))
    return jax.shard_map(
        per_device, mesh=mesh, in_specs=placed, out_specs=P(("op", "cd"), "vp"), check_vma=False
    )
```

```python
import functools

import jax
import jax.numpy as jnp
from jax import lax
from jax.experimental import pallas as pl
from jax.experimental.pallas import tpu as pltpu
from jax.sharding import PartitionSpec as P

LANES = 128
AB_TILE = 256
CONTRACT_TILE = 1024
IRREPS = 8
OFF, N_LOW, COL0, COL1, COL2, TILE = 0, 1, 2, 3, 4, 5


def position():
    z = lax.axis_index("vp")
    core = lax.axis_index("cd") & 1
    return z, core, 1 - 2 * core


def prepare_kernel(owners, win_tiles, ab_ref, cd_ref, w_ref, scal, hi, lo, below):
    step = pl.program_id(0)
    width = w_ref.shape[1]
    n_cd_tiles = cd_ref.shape[0]
    per_owner = ab_ref.shape[0] // owners

    @pl.when(step == 0)
    def count():
        z, core, d = position()

        def total(mask):
            return jnp.sum(jnp.where(mask, 1.0, 0.0)).astype(jnp.int32)

        labels = cd_ref[...]
        below[0] = jnp.int32(0)
        below[IRREPS] = jnp.int32(n_cd_tiles * LANES)
        for r in range(1, IRREPS):
            below[r] = total(labels < r)

        def low_of(v):
            rows = ab_ref[pl.ds(pl.multiple_of(v * per_owner, per_owner), per_owner)]
            return jnp.min(rows.astype(jnp.float32)).astype(jnp.int32), rows

        def start_of(low):
            start = jnp.minimum(below[low], n_cd_tiles * LANES - width)
            return start, jnp.minimum(start // LANES, n_cd_tiles - win_tiles)

        low, rows = low_of(z)
        start, tile = start_of(low)
        scal[OFF] = start - tile * LANES
        scal[N_LOW] = total(rows == low)
        scal[COL0] = below[low] - start
        scal[COL1] = below[low + 1] - start
        scal[COL2] = below[low + 2] - start
        scal[TILE] = tile
        for i, k in enumerate((1, -1, 2)):
            scal[TILE + 1 + i] = start_of(low_of((z + k * d + 2 * owners) % owners)[0])[1]

    rows = lax.broadcasted_iota(jnp.int32, (AB_TILE, 1), 0) + step * AB_TILE
    first = jnp.where(rows < scal[N_LOW], scal[COL0], scal[COL1])
    last = jnp.where(rows < scal[N_LOW], scal[COL1], scal[COL2])
    for at in range(0, width, LANES):
        cols = lax.broadcasted_iota(jnp.int32, (AB_TILE, LANES), 1) + at
        w = jnp.where((cols >= first) & (cols < last), w_ref[:, at : at + LANES], 0.0)
        high = w.astype(jnp.bfloat16)
        hi[:, at : at + LANES] = high
        lo[:, at : at + LANES] = (w - high.astype(jnp.float32)).astype(jnp.bfloat16)


def prepare(irrep_ab, irrep_cd, w_slab, owners):
    ab, width = w_slab.shape
    labels_ab = irrep_ab.reshape(-1, LANES)
    labels_cd = irrep_cd.reshape(-1, LANES)
    tile_spec = pl.BlockSpec((AB_TILE, width), lambda i: (i, 0))
    half = jax.ShapeDtypeStruct((ab, width), jnp.bfloat16)
    return pl.pallas_call(
        functools.partial(prepare_kernel, owners, width // LANES + 1),
        grid=(ab // AB_TILE,),
        in_specs=[
            pl.BlockSpec(labels_ab.shape, lambda i: (0, 0)),
            pl.BlockSpec(labels_cd.shape, lambda i: (0, 0)),
            tile_spec,
        ],
        out_specs=[pl.BlockSpec(memory_space=pltpu.SMEM), tile_spec, tile_spec],
        out_shape=[jax.ShapeDtypeStruct((16,), jnp.int32), half, half],
        scratch_shapes=[pltpu.SMEM((16,), jnp.int32)],
        compiler_params=pltpu.CompilerParams(vmem_limit_bytes=16 * 1024 * 1024),
        cost_estimate=pl.CostEstimate(flops=8 * ab * width, bytes_accessed=8 * ab * width, transcendentals=0),
    )(labels_ab, labels_cd, w_slab)


def gate_kernel(scal, block, out):
    pass


def after(scal, block):
    vmem = pl.BlockSpec(memory_space=pltpu.VMEM)
    return pl.pallas_call(
        gate_kernel,
        in_specs=[pl.BlockSpec(memory_space=pltpu.SMEM), vmem],
        out_specs=vmem,
        out_shape=jax.ShapeDtypeStruct(block.shape, block.dtype),
        input_output_aliases={1: 0},
        compiler_params=pltpu.CompilerParams(vmem_limit_bytes=2 * 1024 * 1024),
    )(scal, block)


def cut_kernel(picks, n_src, scal, *refs):
    srcs, outs = refs[:n_src], refs[n_src:]
    for out, (place, chosen) in zip(outs, picks):
        at = scal[TILE + place]
        for i, s in enumerate(chosen):
            out[i] = srcs[s][:, pl.ds(at, out.shape[2])]


def cut(scal, sources, picks, win_tiles):
    groups, _, _, _ = sources[0].shape
    outs = [jax.ShapeDtypeStruct((len(p[1]), groups, win_tiles, 8, LANES), jnp.float32) for p in picks]
    vmem = pl.BlockSpec(memory_space=pltpu.VMEM)
    size = sum(4 * o.size for o in outs)
    return pl.pallas_call(
        functools.partial(cut_kernel, picks, len(sources)),
        in_specs=[pl.BlockSpec(memory_space=pltpu.SMEM)] + [vmem] * len(sources),
        out_specs=[vmem] * len(outs),
        out_shape=outs,
        compiler_params=pltpu.CompilerParams(vmem_limit_bytes=8 * 1024 * 1024),
        cost_estimate=pl.CostEstimate(flops=0, bytes_accessed=2 * size, transcendentals=0),
    )(scal, *sources)


def contract_kernel(rels, shapes, carried, scal, *refs):
    n_src = len(shapes)
    srcs, refs = refs[:n_src], refs[n_src:]
    w_hi, w_lo, refs = refs[0], refs[1], refs[2:]
    if carried:
        refs = refs[2:]
    mine, other, amps = refs
    width = w_hi.shape[1]
    padded = amps.shape[1] // 2
    tiles = width // LANES
    share = mine.shape[1]

    off, tile0 = scal[OFF], scal[TILE]
    lane = lax.broadcasted_iota(jnp.int32, (padded, LANES), 1)
    keep = lane < LANES - off
    turn = lax.rem(LANES - off, LANES)
    rolled = None
    for j in range(tiles + 1):
        pieces = []
        for ref, count in zip(srcs, shapes):
            if count is None:
                pieces.append(ref[:, pl.ds(tile0 + j, 1)].reshape(share, LANES))
            else:
                pieces += [ref[i, :, j].reshape(share, LANES) for i in range(count)]
        if padded > share * len(rels):
            pieces.append(jnp.zeros((padded - share * len(rels), LANES), jnp.float32))
        new = pltpu.roll(jnp.concatenate(pieces, axis=0), turn, 1)
        if rolled is not None:
            value = jnp.where(keep, rolled, new).T
            high = value.astype(jnp.bfloat16)
            rows = slice((j - 1) * LANES, j * LANES)
            amps[rows, :padded] = high
            amps[rows, padded:] = (value - high.astype(jnp.float32)).astype(jnp.bfloat16)
        rolled = new

    dot = functools.partial(jnp.dot, preferred_element_type=jnp.float32)
    z, core, d = position()
    for at in range(0, w_hi.shape[0], CONTRACT_TILE):
        cols = slice(at, at + CONTRACT_TILE)
        both = dot(w_hi[cols], amps[...])
        turned = both[:, :padded] + both[:, padded:] + dot(w_lo[cols], amps[:, :padded])
        out = turned.T
        for i, rel in enumerate(rels):
            block = (z + rel * d + 32) & 15
            value = out[i * share : (i + 1) * share]

            @pl.when((block & 1) == core)
            def keep_block():
                mine[pl.ds(block >> 1, 1), :, cols] = value[None]

            @pl.when((block & 1) != core)
            def send_block():
                other[pl.ds(block >> 1, 1), :, cols] = value[None]


def contract(scal, sources, rels, w_hi, w_lo, old=()):
    ab, width = w_hi.shape
    shapes = [None if s.ndim == 4 else s.shape[0] for s in sources]
    share = 16
    rows = share * len(rels)
    padded = -(-rows // LANES) * LANES
    vmem = pl.BlockSpec(memory_space=pltpu.VMEM)
    out_shape = jax.ShapeDtypeStruct((8, share, ab), jnp.float32)
    n_in = len(sources) + 3
    return pl.pallas_call(
        functools.partial(contract_kernel, rels, shapes, bool(old)),
        in_specs=[pl.BlockSpec(memory_space=pltpu.SMEM)] + [vmem] * (n_in - 1 + len(old)),
        out_specs=[vmem, vmem],
        out_shape=[out_shape, out_shape],
        input_output_aliases={n_in: 0, n_in + 1: 1} if old else {},
        scratch_shapes=[pltpu.VMEM((width, 2 * padded), jnp.bfloat16)],
        compiler_params=pltpu.CompilerParams(vmem_limit_bytes=20 * 1024 * 1024),
        cost_estimate=pl.CostEstimate(
            flops=rows * width * ab // 8, bytes_accessed=ab * width, transcendentals=0
        ),
    )(scal, *sources, w_hi, w_lo, *old)


def reduce_rows(mine, other):
    n_cd = lax.axis_size("cd")
    pair = [(i, i ^ 1) for i in range(n_cd)]
    both = mine + lax.ppermute(other, "cd", pair)
    groups = [[c for c in range(n_cd) if c % 2 == p] for p in range(2)]
    parts = lax.all_to_all(both, "cd", 0, 0, axis_index_groups=groups)
    return jnp.sum(parts, axis=0)


def per_device(t2_amps, w_slab, irrep_ab, irrep_cd):
    n_vp = lax.axis_size("vp")
    n_cd = lax.axis_size("cd")
    rows_dev, cd_dev = t2_amps.shape
    win_tiles = w_slab.shape[1] // LANES + 1

    def move(array, k):
        pairs = [
            (v * n_cd + e, ((v + (k if e % 2 == 0 else -k)) % n_vp) * n_cd + e)
            for v in range(n_vp)
            for e in range(n_cd)
        ]
        return lax.ppermute(array, ("vp", "cd"), pairs)

    own = t2_amps.reshape(rows_dev // 8, 8, cd_dev // LANES, LANES).transpose(0, 2, 1, 3)
    x1 = move(own, 3)
    y1 = move(own, -3)
    scal, w_hi, w_lo = prepare(irrep_ab, irrep_cd, w_slab, n_vp)
    x1 = after(scal, x1)
    x2 = move(x1, 3)
    y2 = move(y1, -3)
    to_x, to_y = cut(scal, [own, x1, y1], [(1, (0, 1, 2)), (2, (0, 1, 2))], win_tiles)
    near_x = move(to_x, 1)
    near_y = move(to_y, -1)
    to_x, to_y, to_edge = cut(scal, [x2, y2], [(1, (0, 1)), (2, (0, 1)), (3, (0,))], win_tiles)
    far_x = move(to_x, 1)
    far_y = move(to_y, -1)
    edge = move(to_edge, 2)
    first = contract(
        scal,
        [own, x1, y1, x2, y2, near_x, near_y],
        [0, -3, 3, -6, 6, -1, -4, 2, 1, -2, 4],
        w_hi,
        w_lo,
    )
    mine, other = contract(scal, [far_x, far_y, edge], [-7, 5, -5, 7, -8], w_hi, w_lo, first)
    return reduce_rows(mine, other)


def solution(mesh):
    placed = (P(("op", "vp"), "cd"), P("vp", "cd"), P(), P("cd"))
    return jax.shard_map(
        per_device, mesh=mesh, in_specs=placed, out_specs=P(("op", "cd"), "vp"), check_vma=False
    )
```
